256 devices in a mesh: dp: 16 (over y, x), expert: 16 (over z, core).
Axes of the slice: x: 4, y: 4, z: 8, core: 2. Of those that a mesh axis runs over, the one named last changes fastest.
Arguments:
- out_grad: bfloat16 [32768, 3584], P(('dp', 'expert')), may hold values from -1.5 to 1.5
- route_ids: int32 [32768, 2], P(('dp', 'expert')), may hold values from 0 to 15, all different within a row; in each aligned block of 128 rows (0 to 127, 128 to 255, ...) at most 24 rows name the same one
- route_weights: bfloat16 [32768, 2], P(('dp', 'expert')), may hold values from 0.099609375 to 1
- saved_gate_up: bfloat16 [256, 384, 2048], P(('dp', 'expert')), may hold values from -6 to 6
- down_weight: bfloat16 [16, 1024, 3584], P('expert'), may hold values from -0.1875 to 0.1875
Outputs:
- grad_gate_up: bfloat16 [256, 384, 2048], P(('dp', 'expert'))
- grad_weight: bfloat16 [16, 1024, 3584], P('expert', 'dp')
- weight_scales: float32 [16, 32, 3584], P('expert', 'dp')
- grad_route: float32 [32768, 2], P(('dp', 'expert'))
The draws below stay inside these ranges and needn't reach their ends.
Inputs may be any that keep to these rules, and one draw needn't show every extreme that they name: `route_ids`: each token names 2 different experts. Within the 128 tokens of one device no expert is named by more than 24 tokens, and in every draw some device's block names some expert exactly 24 times.
All inputs are finite; a program needn't handle non-finite values.
Results may differ from the reference program's by a relative error of at most 0.02.
Values may be sent and summed in bfloat16 or wider, within the bound.
A program may use at most 128 MiB of HBM per device.

```python
import math
import jax
import jax.numpy as jnp
import numpy as np
from jax import lax

D = 3584
FF = 1024
TOPW = 2
TOK_DEV = 128
EXPERTS = 16
CAP = 24
TOKENS = 32768
N_DP = 16
N_EXPERT = 16


def block_levels(rng, shape, pieces, smallest, top_value):
    def one(dim, parts):
        steps = jax.random.uniform(jax.random.fold_in(jax.random.fold_in(rng, 6), dim), (parts,), jnp.float32, smallest / len(pieces), top_value / len(pieces))
        return jnp.repeat(jnp.exp(steps), shape[dim] // parts).reshape((-1,) + (1,) * (len(shape) - dim - 1))

    factor_of = one(*pieces[0])
    for cut in pieces[1:]:
        factor_of = factor_of * one(*cut)
    return factor_of


def routed_block(key, own, number, rows, count, top, most, lean):
    sequence = jax.random.permutation(key, count)
    crowded, common = load_shares(count, rows * top, most, lean, True), load_shares(count, rows * top, most, lean, False)
    places = jnp.arange(count)

    def named(lengths, turn):
        used = int((lengths > 0).sum())
        fixed = max(1, used // 4)
        passed = fixed + (places - fixed + turn * (used - fixed)) % max(1, count - fixed)
        return jnp.zeros((count,), jnp.int32).at[sequence[jnp.where(places < fixed, places, passed)]].set(jnp.asarray(lengths, jnp.int32))

    lengths = jnp.where(number % 4 == 0, named(crowded, number // 4), named(common, number - number // 4 - 1))
    mixed = jax.random.permutation(jax.random.fold_in(own, 3), count)
    giver, taker = mixed[0:count // 2 * 2:2], mixed[1:count // 2 * 2:2]
    slack = jnp.minimum(lengths[giver] - 1, most - lengths[taker]) // 2
    slack = jnp.where((giver == sequence[0]) | (taker == sequence[0]) | (lengths[taker] == 0), 0, jnp.maximum(slack, 0))
    passed = jax.random.randint(jax.random.fold_in(own, 4), (count // 2,), 0, 1 << 20) % (slack + 1)
    lengths = lengths.at[giver].add(-passed).at[taker].add(passed)
    items = jnp.searchsorted(jnp.cumsum(lengths), jnp.arange(rows * top), side="right").astype(jnp.int32)
    table = items.reshape(top, rows).T
    table = table[jax.random.permutation(jax.random.fold_in(own, 1), rows)]
    turn = jax.random.randint(jax.random.fold_in(own, 2), (rows, 1), 0, top)
    return jnp.take_along_axis(table, (jnp.arange(top)[None, :] + turn) % top, axis=1)


def load_shares(amount, total, reach, lean, full):
    loads = [(1 << 20) // math.isqrt(rank ** lean) + 1 for rank in range(1, amount + 1)]
    largest = reach if full else min(reach, max(-(-total // amount), total * loads[0] // sum(loads)))
    least = 1 if total - largest >= amount - 1 else 0
    given, surplus = [largest] + [least] * (amount - 1), total - largest - least * (amount - 1)
    while surplus > 0:
        candidates = [i for i in range(1, amount) if given[i] < largest] or [i for i in range(1, amount) if given[i] < reach]
        whole, budget = sum([loads[i] for i in candidates]), surplus
        for i in candidates:
            addition = min(reach - given[i], max(1, budget * loads[i] // whole), surplus)
            given[i] = given[i] + addition
            surplus = surplus - addition
    return np.array(given)


def centred(own_key, extent, spread, bound, pieces=(), held_as=jnp.bfloat16):
    drawn = jax.random.normal(own_key, extent, jnp.float32) * spread
    if len(pieces) > 0:
        drawn = block_levels(own_key, extent, pieces, -0.22, 0.18) * drawn
    return jnp.clip(drawn, min=-bound, max=bound).astype(held_as)


def setup_inputs(seed: int = 0) -> dict:
    key_of = jax.random.split(jax.random.key(seed), 6)
    out_grad = centred(key_of[0], (TOKENS, D), 0.25, 1.5, ((0, 256),))
    route_ids_keys = jax.random.split(jax.random.fold_in(key_of[1], 1), TOKENS // TOK_DEV)
    route_ids_turns = jax.random.permutation(jax.random.fold_in(key_of[1], 3), TOKENS // TOK_DEV)
    route_ids = jax.vmap(lambda own, number: routed_block(jax.random.fold_in(key_of[1], 2), own, number, TOK_DEV, EXPERTS, TOPW, CAP, 2))(route_ids_keys, route_ids_turns).reshape((TOKENS, TOPW))
    route_weights = jnp.clip(0.099609375 + 0.9003906 * jax.random.uniform(key_of[2], (TOKENS, TOPW), jnp.float32) ** block_levels(key_of[2], (TOKENS, TOPW), ((0, 256),), -0.2, 0.2), 0.099609375, 1.0).astype(jnp.bfloat16)
    saved_gate_up = centred(key_of[3], (N_DP * EXPERTS, EXPERTS * CAP, 2 * FF), 1.0, 6.0, ((0, 256),))
    down_weight = centred(key_of[4], (EXPERTS, FF, D), FF ** -0.5, 0.1875, ((0, 16),))
    return dict(out_grad=out_grad, route_ids=route_ids, route_weights=route_weights, saved_gate_up=saved_gate_up, down_weight=down_weight)


tiny_scale = 1e-6


def route_slots(route_ids):
    pick_count = TOK_DEV * TOPW
    flat_ids = route_ids.reshape(N_DP, N_EXPERT, pick_count)
    onehot = (flat_ids[..., None] == jnp.arange(EXPERTS, dtype=jnp.int32)).astype(jnp.int32)
    slot_rank = jnp.sum((jnp.cumsum(onehot, axis=2) - 1) * onehot, axis=3)
    return (flat_ids * CAP + slot_rank).astype(jnp.int32)


def reference(out_grad, route_ids, route_weights, saved_gate_up, down_weight):
    pick_count = TOK_DEV * TOPW
    slot_count = EXPERTS * CAP
    slot_index = route_slots(route_ids)
    pick_ids = jnp.arange(pick_count, dtype=jnp.int32)

    def fill_table(index_row):
        return jnp.full((slot_count,), -1, jnp.int32).at[index_row].set(pick_ids)

    slot_table = jax.vmap(jax.vmap(fill_table))(slot_index)
    grad_tokens = out_grad.reshape(N_DP, N_EXPERT, TOK_DEV, D)
    pick_weights = route_weights.reshape(N_DP, N_EXPERT, pick_count)
    saved = saved_gate_up.reshape(N_DP, N_EXPERT, slot_count, 2 * FF)

    def one_expert(expert_id):
        chosen = lax.dynamic_slice_in_dim(slot_table, expert_id * CAP, CAP, 2)
        present = chosen >= 0
        safe_pick = jnp.maximum(chosen, 0).astype(jnp.int32)
        token_row = (safe_pick // TOPW).astype(jnp.int32)
        gathered = jnp.take_along_axis(grad_tokens, token_row[..., None], axis=2)
        grad_rows = jnp.where(present[..., None], gathered, jnp.zeros_like(gathered))
        row_weights = jnp.take_along_axis(pick_weights, safe_pick, axis=2).astype(jnp.float32)
        row_weights = jnp.where(present, row_weights, jnp.zeros_like(row_weights))
        flat_rows = grad_rows.reshape(N_DP * slot_count, D)
        flat_weights = row_weights.reshape(N_DP * slot_count)
        gate_up = lax.dynamic_index_in_dim(saved, expert_id, 1, keepdims=False)
        weight_mat = lax.dynamic_index_in_dim(down_weight, expert_id, 0, keepdims=False)
        weighted = (flat_weights[:, None] * flat_rows.astype(jnp.float32)).astype(jnp.bfloat16)
        gate_pre = gate_up[..., :FF].reshape(N_DP * slot_count, FF).astype(jnp.float32)
        up_pre = gate_up[..., FF:].reshape(N_DP * slot_count, FF).astype(jnp.float32)
        sigmoid_gate = jax.nn.sigmoid(gate_pre)
        hidden_act = (gate_pre * sigmoid_gate * up_pre).astype(jnp.bfloat16)
        expert_out = jnp.dot(hidden_act, weight_mat, preferred_element_type=jnp.float32)
        route_part = jnp.sum(flat_rows.astype(jnp.float32) * expert_out, axis=1)
        grad_act = jnp.dot(weighted, weight_mat.T, preferred_element_type=jnp.float32)
        grad_gate = grad_act * up_pre * sigmoid_gate * (1.0 + gate_pre * (1.0 - sigmoid_gate))
        grad_up = grad_act * gate_pre * sigmoid_gate
        grad_pair = jnp.concatenate([grad_gate, grad_up], axis=1).astype(jnp.bfloat16)
        partial_value = jnp.einsum("nrf,nrd->nfd",
                             hidden_act.reshape(N_DP, slot_count, FF).astype(jnp.float32),
                             weighted.reshape(N_DP, slot_count, D).astype(jnp.float32))
        block_max = jnp.max(jnp.abs(partial_value).reshape(N_DP, FF // 32, 32, D), axis=2)
        scales = jnp.max(block_max, axis=0) + tiny_scale
        scaled = (partial_value / jnp.repeat(scales, 32, axis=0)[None]).astype(jnp.bfloat16)
        scaled = lax.optimization_barrier(scaled)
        grad_weight = jnp.sum(scaled.astype(jnp.float32), axis=0).astype(jnp.bfloat16)
        return (grad_pair.reshape(N_DP, slot_count, 2 * FF), grad_weight, scales,
                route_part.reshape(N_DP, N_EXPERT, CAP))

    per_expert = lax.map(one_expert, jnp.arange(EXPERTS, dtype=jnp.int32))
    grad_pairs, grad_weight, weight_scales, route_all = per_expert
    grad_gate_up = jnp.transpose(grad_pairs, (1, 0, 2, 3)).reshape(N_DP * EXPERTS, slot_count, 2 * FF)
    route_table = jnp.transpose(route_all, (1, 2, 0, 3)).reshape(N_DP, N_EXPERT, slot_count)
    grad_route = jnp.take_along_axis(route_table, slot_index, axis=2).reshape(TOKENS, TOPW)
    return grad_gate_up, grad_weight, weight_scales, grad_route
```

```python
import functools

import jax
import jax.numpy as jnp
from jax import lax
from jax.experimental import pallas as pl
from jax.experimental.pallas import tpu as pltpu
from jax.sharding import PartitionSpec as P

MESH = pl.DeviceIdType.MESH
F32, BF16 = jnp.float32, jnp.bfloat16
TINY = 1e-06
COLS = 256
AHEAD = 4
LAG1, LAG2 = 2, 2
Z, SIDE = 8, 4


def kernel(
    ids_ref, gate_ref, og_hbm, saved_hbm, w_hbm,
    ggu_hbm, gw_ref, ws_ref, gr_ref,
    og, saved, wmat, smat, rank_s, zsend, zrecv, wsend, wrecv, wrep, hid, hid_t,
    gact, racc, part, s1r, s2s, s2m, s2r, s2mr, rsend, rrecv, ggu,
    in_sem, w_sem, zs_sem, zr_sem, ws_sem, wr_sem, s1s_sem, s1r_sem,
    s2s_sem, s2r_sem, m2s_sem, m2r_sem, rs_sem, rr_sem, out_sem,
):
    chunks = zrecv.shape[0]
    experts, cap = zrecv.shape[1], zrecv.shape[2]
    slots, hidden = hid.shape
    dp, me = lax.axis_index("dp"), lax.axis_index("expert")
    y, x = dp // SIDE, lax.rem(dp, SIDE)
    z, core = me // 2, lax.rem(me, 2)
    quarter = hidden // SIDE
    share = quarter // SIDE

    zpeers = []
    for dz in (4, 3, 5, 2, 6, 1, 7, 0):
        for dc in (0, 1):
            if dz or dc:
                zpeers.append(lax.rem(z + dz, Z) * 2 + lax.rem(core + dc, 2))

    def along(axis, step):
        return lax.rem(y + step * (1 - axis), SIDE) * SIDE + lax.rem(x + step * axis, SIDE)

    def place(axis):
        return y * (1 - axis) + x * axis

    load_og = pltpu.make_async_copy(og_hbm, og, in_sem.at[0])
    load_saved = pltpu.make_async_copy(saved_hbm.at[0], saved, in_sem.at[1])

    def load_w(c):
        cols = pl.ds(pl.multiple_of(c * COLS, COLS), COLS)
        return pltpu.make_async_copy(w_hbm.at[0, :, cols], wmat.at[c], w_sem.at[c])

    load_og.start()
    load_saved.start()

    barrier = pltpu.get_barrier_semaphore()
    for e in zpeers:
        pl.semaphore_signal(barrier, inc=1, device_id=(dp, e), device_id_type=MESH)
    for step in (1, 2, 3):
        for axis in (0, 1):
            pl.semaphore_signal(barrier, inc=1, device_id=(along(axis, step), me), device_id_type=MESH)

    ids = ids_ref[...]
    tokens = ids.shape[1]
    gates = gate_ref[...].astype(F32)
    e_iota = lax.broadcasted_iota(jnp.int32, (experts, tokens), 0)
    first = (ids[0:1] == e_iota).astype(F32)
    second = (ids[1:2] == e_iota).astype(F32)
    named = first + second
    gate_of = first * gates[0:1] + second * gates[1:2]
    earlier = (
        lax.broadcasted_iota(jnp.int32, (tokens, tokens), 0)
        < lax.broadcasted_iota(jnp.int32, (tokens, tokens), 1)
    ).astype(F32).astype(BF16)
    rank = jnp.dot(named.astype(BF16), earlier, preferred_element_type=F32)
    rank = jnp.where(named > 0.5, rank, -1.0)
    rank_s[...] = rank
    c_iota = lax.broadcasted_iota(jnp.int32, (cap, tokens), 0).astype(F32)
    rows = []
    for e in range(experts):
        pick = jnp.where(rank[e:e + 1] == c_iota, 1.0, 0.0)
        rows.append(pick)
        gate_row = jnp.sum(pick * gate_of[e:e + 1], axis=1, keepdims=True)
        wsend[e] = jnp.broadcast_to(gate_row, (cap, 128)).astype(BF16)
    smat[...] = jnp.concatenate(rows, axis=0).astype(BF16)
    wrecv[me] = wsend[me]

    pl.semaphore_wait(barrier, len(zpeers) + 6)
    for e in zpeers:
        pltpu.make_async_remote_copy(
            src_ref=wsend.at[e], dst_ref=wrecv.at[me], send_sem=ws_sem, recv_sem=wr_sem,
            device_id=(dp, e), device_id_type=MESH,
        ).start()
    load_og.wait()

    def produce(c):
        cols = pl.ds(pl.multiple_of(c * COLS, COLS), COLS)
        block = jnp.dot(smat[...], og[:, cols], preferred_element_type=F32)
        zsend[c] = block.reshape(experts, cap, COLS).astype(BF16)
        zrecv[c, me] = zsend[c, me]
        for e in zpeers:
            pltpu.make_async_remote_copy(
                src_ref=zsend.at[c, e], dst_ref=zrecv.at[c, me],
                send_sem=zs_sem.at[c], recv_sem=zr_sem.at[c],
                device_id=(dp, e), device_id_type=MESH,
            ).start()
        load_w(c).start()

    lax.fori_loop(0, AHEAD, lambda c, _: (produce(c), 0)[1], 0)

    load_saved.wait()
    slab = 128

    def activate(i, _):
        at = pl.ds(pl.multiple_of(i * slab, slab), slab)
        gate = saved[at, :hidden].astype(F32)
        up = saved[at, hidden:].astype(F32)
        act = gate * jax.nn.sigmoid(gate) * up
        hid[at, :] = act.astype(BF16)
        hid_t[0, :, at] = act.T.astype(BF16)
        return 0

    lax.fori_loop(0, slots // slab, activate, 0)
    for a in range(SIDE):
        for b in range(SIDE):
            hid_t[1, pl.ds((b * SIDE + a) * share, share), :] = hid_t[0, pl.ds((a * SIDE + b) * share, share), :]
    gact[...] = jnp.zeros_like(gact)
    racc[...] = jnp.zeros_like(racc)

    def all_of(ref, sem):
        return pltpu.make_async_copy(ref, ref, sem)

    all_of(wrecv.at[pl.ds(0, experts - 1)], wr_sem).wait()
    wrep[...] = wrecv[...].astype(F32).reshape(slots, 128)

    def work(c):
        axis = lax.rem(c, 2)
        all_of(zrecv.at[c, pl.ds(0, experts - 1)], zr_sem.at[c]).wait()
        load_w(c).wait()
        rows = zrecv[c].astype(F32).reshape(slots, COLS)
        weight = wrep[...]
        weighted = (rows * jnp.concatenate([weight] * (COLS // 128), axis=1)).astype(BF16)
        for k in (1, 2, 3, 0):
            q = lax.rem(place(axis) + k, SIDE)
            lhs = hid_t[axis, pl.ds(pl.multiple_of(q * quarter, quarter), quarter), :]
            part[c, q] = jnp.dot(lhs, weighted, preferred_element_type=F32).astype(BF16)
            if k:
                pltpu.make_async_remote_copy(
                    src_ref=part.at[c, q], dst_ref=s1r.at[c, k - 1],
                    send_sem=s1s_sem.at[c], recv_sem=s1r_sem.at[c],
                    device_id=(along(axis, k), me), device_id_type=MESH,
                ).start()
        wc = wmat[c]
        out = jnp.dot(hid[...], wc, preferred_element_type=F32) * rows
        total = racc[...]
        for i in range(COLS // 128):
            total = total + out[:, i * 128:(i + 1) * 128]
        racc[...] = total
        gact[...] += lax.dot_general(weighted, wc, (((1,), (1,)), ((), ())), preferred_element_type=F32)

    def sum_first(c):
        axis = lax.rem(c, 2)
        mine, other = place(axis), place(1 - axis)
        all_of(s1r.at[c], s1r_sem.at[c]).wait()
        for k in (1, 2, 3, 0):
            q = lax.rem(other + k, SIDE)
            at = pl.ds(pl.multiple_of(q * share, share), share)
            total = part[c, mine, at, :].astype(F32)
            top = jnp.abs(total)
            for i in range(SIDE - 1):
                term = s1r[c, i, at, :].astype(F32)
                total = total + term
                top = jnp.maximum(top, jnp.abs(term))
            s2s[c, q] = total.astype(BF16)
            s2m[c, q] = jnp.max(top.reshape(share // 32, 32, COLS), axis=1)
            if k:
                peer = (along(1 - axis, k), me)
                pltpu.make_async_remote_copy(
                    src_ref=s2s.at[c, q], dst_ref=s2r.at[c, k - 1],
                    send_sem=s2s_sem.at[c], recv_sem=s2r_sem.at[c],
                    device_id=peer, device_id_type=MESH,
                ).start()
                pltpu.make_async_remote_copy(
                    src_ref=s2m.at[c, q], dst_ref=s2mr.at[c, k - 1],
                    send_sem=m2s_sem.at[c], recv_sem=m2r_sem.at[c],
                    device_id=peer, device_id_type=MESH,
                ).start()

    def sum_second(c):
        axis = lax.rem(c, 2)
        other = place(1 - axis)
        cols = pl.ds(pl.multiple_of(c * COLS, COLS), COLS)
        all_of(s2r.at[c], s2r_sem.at[c]).wait()
        all_of(s2mr.at[c], m2r_sem.at[c]).wait()
        total = s2s[c, other].astype(F32)
        top = s2m[c, other]
        for i in range(SIDE - 1):
            total = total + s2r[c, i].astype(F32)
            top = jnp.maximum(top, s2mr[c, i])
        scale = top + TINY
        ws_ref[0, :, cols] = scale
        parts = []
        for b in range(share // 32):
            parts.append(total[b * 32:(b + 1) * 32] / scale[b:b + 1])
        gw_ref[0, :, cols] = jnp.concatenate(parts, axis=0).astype(BF16)

    def step(c, _):
        @pl.when(c + AHEAD < chunks)
        def _():
            produce(c + AHEAD)

        work(c)

        @pl.when(c >= LAG1)
        def _():
            sum_first(c - LAG1)

        @pl.when(c >= LAG1 + LAG2)
        def _():
            sum_second(c - LAG1 - LAG2)

        return 0

    lax.fori_loop(0, chunks, step, 0)

    route = jnp.broadcast_to(jnp.sum(racc[...], axis=1, keepdims=True), (slots, 128))
    rsend[...] = route.reshape(experts, cap, 128)
    rrecv[me] = rsend[me]
    for e in zpeers:
        pltpu.make_async_remote_copy(
            src_ref=rsend.at[e], dst_ref=rrecv.at[me], send_sem=rs_sem, recv_sem=rr_sem,
            device_id=(dp, e), device_id_type=MESH,
        ).start()

    def finish(i, _):
        at = pl.ds(pl.multiple_of(i * slab, slab), slab)
        gate = saved[at, :hidden].astype(F32)
        up = saved[at, hidden:].astype(F32)
        sg = jax.nn.sigmoid(gate)
        ga = gact[at, :]
        ggu[at, :hidden] = (ga * up * sg * (1.0 + gate * (1.0 - sg))).astype(BF16)
        ggu[at, hidden:] = (ga * gate * sg).astype(BF16)
        return 0

    lax.fori_loop(0, slots // slab, finish, 0)
    store_ggu = pltpu.make_async_copy(ggu, ggu_hbm.at[0], out_sem)
    store_ggu.start()

    lax.fori_loop(chunks - LAG1, chunks, lambda c, _: (sum_first(c), 0)[1], 0)

    all_of(rrecv.at[pl.ds(0, experts - 1)], rr_sem).wait()
    ids = ids_ref[...]
    rank = rank_s[...]
    e_iota = lax.broadcasted_iota(jnp.int32, (experts, tokens), 0)
    c_iota = lax.broadcasted_iota(jnp.int32, (cap, tokens), 0).astype(F32)
    got = []
    for e in range(experts):
        got.append(jnp.sum(jnp.where(rank[e:e + 1] == c_iota, rrecv[e], 0.0), axis=0, keepdims=True))
    got = jnp.concatenate(got, axis=0)
    for k in range(2):
        gr_ref[k:k + 1, :] = jnp.sum(jnp.where(ids[k:k + 1] == e_iota, got, 0.0), axis=0, keepdims=True)

    lax.fori_loop(chunks - LAG1 - LAG2, chunks, lambda c, _: (sum_second(c), 0)[1], 0)

    store_ggu.wait()
    all_of(wsend.at[pl.ds(0, experts - 1)], ws_sem).wait()
    all_of(rsend.at[pl.ds(0, experts - 1)], rs_sem).wait()

    def drain(c, _):
        all_of(zsend.at[c, pl.ds(0, experts - 1)], zs_sem.at[c]).wait()
        all_of(s1r.at[c], s1s_sem.at[c]).wait()
        all_of(s2r.at[c], s2s_sem.at[c]).wait()
        all_of(s2mr.at[c], m2s_sem.at[c]).wait()
        return 0

    lax.fori_loop(0, chunks, drain, 0)


def shards(out_grad, route_ids, route_weights, saved_gate_up, down_weight):
    tokens, width = out_grad.shape
    hidden = down_weight.shape[1]
    experts = lax.axis_size("expert")
    slots = saved_gate_up.shape[1]
    cap = slots // experts
    chunks = width // COLS
    quarter, share = hidden // SIDE, hidden // SIDE // SIDE
    hbm, vmem = pl.BlockSpec(memory_space=pl.ANY), pl.BlockSpec(memory_space=pltpu.VMEM)
    dma = pltpu.SemaphoreType.DMA
    ggu, gw, ws, gr = pl.pallas_call(
        kernel,
        out_shape=(
            jax.ShapeDtypeStruct((1, slots, 2 * hidden), BF16),
            jax.ShapeDtypeStruct((1, share, width), BF16),
            jax.ShapeDtypeStruct((1, share // 32, width), F32),
            jax.ShapeDtypeStruct((2, tokens), F32),
        ),
        in_specs=[vmem, vmem, hbm, hbm, hbm],
        out_specs=(hbm, vmem, vmem, vmem),
        scratch_shapes=[
            pltpu.VMEM((tokens, width), BF16),
            pltpu.VMEM((slots, 2 * hidden), BF16),
            pltpu.VMEM((chunks, hidden, COLS), BF16),
            pltpu.VMEM((slots, tokens), BF16),
            pltpu.VMEM((experts, tokens), F32),
            pltpu.VMEM((chunks, experts, cap, COLS), BF16),
            pltpu.VMEM((chunks, experts, cap, COLS), BF16),
            pltpu.VMEM((experts, cap, 128), BF16),
            pltpu.VMEM((experts, cap, 128), BF16),
            pltpu.VMEM((slots, 128), F32),
            pltpu.VMEM((slots, hidden), BF16),
            pltpu.VMEM((2, hidden, slots), BF16),
            pltpu.VMEM((slots, hidden), F32),
            pltpu.VMEM((slots, 128), F32),
            pltpu.VMEM((chunks, SIDE, quarter, COLS), BF16),
            pltpu.VMEM((chunks, SIDE - 1, quarter, COLS), BF16),
            pltpu.VMEM((chunks, SIDE, share, COLS), BF16),
            pltpu.VMEM((chunks, SIDE, share // 32, COLS), F32),
            pltpu.VMEM((chunks, SIDE - 1, share, COLS), BF16),
            pltpu.VMEM((chunks, SIDE - 1, share // 32, COLS), F32),
            pltpu.VMEM((experts, cap, 128), F32),
            pltpu.VMEM((experts, cap, 128), F32),
            pltpu.VMEM((slots, 2 * hidden), BF16),
            dma((2,)), dma((chunks,)), dma((chunks,)), dma((chunks,)), dma, dma, dma((chunks,)), dma((chunks,)),
            dma((chunks,)), dma((chunks,)), dma((chunks,)), dma((chunks,)), dma, dma, dma,
        ],
        compiler_params=pltpu.CompilerParams(
            collective_id=0, has_side_effects=True, vmem_limit_bytes=60 * 2**20
        ),
    )(route_ids.T, route_weights.T, out_grad, saved_gate_up, down_weight)
    return ggu, gw, ws, gr.T


def solution(mesh):
    in_specs = (
        P(("dp", "expert"), None),
        P(("dp", "expert"), None),
        P(("dp", "expert"), None),
        P(("dp", "expert"), None, None),
        P("expert", None, None),
    )
    out_specs = (
        P(("dp", "expert"), None, None),
        P("expert", "dp", None),
        P("expert", "dp", None),
        P(("dp", "expert"), None),
    )
    return jax.shard_map(shards, mesh=mesh, in_specs=in_specs, out_specs=out_specs, check_vma=False)
```

```python
import functools

import jax
import jax.numpy as jnp
from jax import lax
from jax.experimental import pallas as pl
from jax.experimental.pallas import tpu as pltpu
from jax.sharding import PartitionSpec as P

MESH = pl.DeviceIdType.MESH
F32, BF16 = jnp.float32, jnp.bfloat16
TINY = 1e-06
COLS, HALF = 256, 128
HOPS, RELAYS = 3, 3
LAG1, LAG2 = 2, 2
Z, SIDE = 8, 4


def kernel(
    ids_ref, gate_ref, og_hbm, saved_hbm, w_hbm,
    ggu, gw_ref, ws_ref, gr_ref,
    og, saved, wmat, s_own, s_side, rank_s, hop, zown, zsend, zrecv, info_s, info, wrep, hid, hid_t,
    gact, racc, part, s1r, s2s, s2m, s2r, s2mr, rsend, rrecv,
    in_sem, w_sem, hs_sem, hr_sem, zs_sem, zr_sem, is_sem, ir_sem, s1s_sem, s1r_sem,
    s2s_sem, s2r_sem, m2s_sem, m2r_sem, rs_sem, rr_sem,
):
    chunks = zrecv.shape[0]
    experts, cap = zrecv.shape[1], zrecv.shape[2]
    slots, hidden = hid.shape
    dp, me = lax.axis_index("dp"), lax.axis_index("expert")
    y, x = dp // SIDE, lax.rem(dp, SIDE)
    z, core = me // 2, lax.rem(me, 2)
    quarter = hidden // SIDE
    share = quarter // SIDE

    def expert_at(dz, other):
        return lax.rem(z + dz + Z, Z) * 2 + (1 - core if other else core)

    zpeers = [expert_at(dz, o) for dz in (1, -1, 2, -2, 3, -3, 4, 0) for o in (0, 1) if dz or o]
    near, others = (zpeers[2], zpeers[0]), zpeers[1:2] + zpeers[3:]
    fills = [
        [expert_at(0, 0), expert_at(0, 1), expert_at(d, 0), expert_at(d, 1),
         expert_at(2 * d, 0), expert_at(2 * d, 1), expert_at(3 * d, d < 0)]
        for d in (1, -1)
    ]
    remote = experts - 3

    def along(axis, step):
        return lax.rem(y + step * (1 - axis), SIDE) * SIDE + lax.rem(x + step * axis, SIDE)

    load_og = pltpu.make_async_copy(og_hbm, og, in_sem.at[0])
    load_saved = pltpu.make_async_copy(saved_hbm.at[0], saved, in_sem.at[1])

    def load_w(c):
        cols = pl.ds(pl.multiple_of(c * COLS, COLS), COLS)
        return pltpu.make_async_copy(w_hbm.at[0, :, cols], wmat.at[c], w_sem.at[c])

    load_og.start()
    load_saved.start()

    barrier = pltpu.get_barrier_semaphore()
    for e in zpeers:
        pl.semaphore_signal(barrier, inc=1, device_id=(dp, e), device_id_type=MESH)
    for step in (1, 2, 3):
        for axis in (0, 1):
            pl.semaphore_signal(barrier, inc=1, device_id=(along(axis, step), me), device_id_type=MESH)

    tokens = ids_ref.shape[1]
    earlier = (
        lax.broadcasted_iota(jnp.int32, (tokens, tokens), 0)
        < lax.broadcasted_iota(jnp.int32, (tokens, tokens), 1)
    ).astype(F32).astype(BF16)
    c_iota = lax.broadcasted_iota(jnp.int32, (cap, tokens), 0).astype(F32)
    e_iota = lax.broadcasted_iota(jnp.int32, (experts, tokens), 0).astype(F32)
    info_s[...] = jnp.zeros_like(info_s)
    info_s[0:2, :] = ids_ref[...].astype(F32)
    info_s[2:4, :] = gate_ref[...].astype(F32)
    info[me] = info_s[...]

    def ranks(named):
        rank = jnp.dot(named.astype(F32).astype(BF16), earlier, preferred_element_type=F32)
        return jnp.where(named, rank, -1.0)

    def picks(rank_row):
        return jnp.where(rank_row == c_iota, 1.0, 0.0)

    def rank_of(i, source):
        first, second = info[source, 0:1, :], info[source, 1:2, :]
        rank_s[i] = ranks((first == e_iota) | (second == e_iota))

    rank_of(2, me)
    s_own[...] = jnp.concatenate([picks(rank_s[2, pl.ds(e, 1), :]) for e in fills[0][:2]], axis=0).astype(BF16)

    pl.semaphore_wait(barrier, len(zpeers) + 6)

    def send_hop(c):
        cols = pl.ds(pl.multiple_of(c * COLS, COLS), COLS)
        for side in (0, 1):
            pltpu.make_async_remote_copy(
                src_ref=og_hbm.at[:, cols], dst_ref=hop.at[c, side],
                send_sem=hs_sem.at[c], recv_sem=hr_sem.at[c, side],
                device_id=(dp, near[1 - side]), device_id_type=MESH,
            ).start()

    def send_info(e):
        pltpu.make_async_remote_copy(
            src_ref=info_s, dst_ref=info.at[me], send_sem=is_sem, recv_sem=ir_sem.at[me],
            device_id=(dp, e), device_id_type=MESH,
        ).start()

    def wait_info(e):
        pltpu.make_async_copy(info.at[e], info.at[e], ir_sem.at[e]).wait()

    send_info(near[0])
    send_info(near[1])
    lax.fori_loop(0, HOPS + RELAYS, lambda c, _: (send_hop(c), 0)[1], 0)
    for e in others:
        send_info(e)
    for side in (0, 1):
        wait_info(near[side])
        rank_of(side, near[side])
        s_side[side] = jnp.concatenate([picks(rank_s[side, pl.ds(e, 1), :]) for e in fills[side]], axis=0).astype(BF16)
    load_og.wait()

    def send_rows(block, c, source, target):
        pltpu.make_async_remote_copy(
            src_ref=block, dst_ref=zrecv.at[c, source],
            send_sem=zs_sem.at[c], recv_sem=zr_sem.at[c],
            device_id=(dp, target), device_id_type=MESH,
        ).start()

    def relay(c):
        cols = pl.ds(pl.multiple_of(c * COLS, COLS), COLS)
        block = jnp.dot(s_own[...], og[:, cols], preferred_element_type=F32)
        block = block.reshape(2, cap, COLS).astype(BF16)
        zrecv[c, me] = block[0]
        zown[c] = block[1]
        send_rows(zown.at[c], c, me, fills[0][1])
        for side in (0, 1):
            pltpu.make_async_copy(hop.at[c, side], hop.at[c, side], hr_sem.at[c, side]).wait()
            block = jnp.dot(s_side[side], hop[c, side], preferred_element_type=F32)
            block = block.reshape(7, cap, COLS).astype(BF16)
            zrecv[c, near[side]] = block[0]
            zsend[c, side] = block
            for i in (6, 4, 5, 2, 3, 1):
                send_rows(zsend.at[c, side, i], c, near[side], fills[side][i])
        load_w(c).start()

    lax.fori_loop(0, RELAYS, lambda c, _: (relay(c), 0)[1], 0)

    load_saved.wait()
    slab = 128

    def activate(i, _):
        at = pl.ds(pl.multiple_of(i * slab, slab), slab)
        gate = saved[at, :hidden].astype(F32)
        up = saved[at, hidden:].astype(F32)
        act = gate * jax.nn.sigmoid(gate) * up
        hid[at, :] = act.astype(BF16)
        hid_t[:, at] = act.T.astype(BF16)
        return 0

    lax.fori_loop(0, slots // slab, activate, 0)
    gact[...] = jnp.zeros_like(gact)
    racc[...] = jnp.zeros_like(racc)

    def all_of(ref, sem):
        return pltpu.make_async_copy(ref, ref, sem)

    for e in others:
        wait_info(e)
    first = jnp.concatenate([info[e, 0:1, :] for e in range(experts)], axis=0)
    second = jnp.concatenate([info[e, 1:2, :] for e in range(experts)], axis=0)
    mine = me.astype(F32)
    rank = ranks((first == mine) | (second == mine))
    for e in range(experts):
        gates = jnp.where(first[e:e + 1] == mine, info[e, 2:3, :], info[e, 3:4, :])
        weight = jnp.sum(picks(rank[e:e + 1]) * gates, axis=1, keepdims=True)
        wrep[e * cap:(e + 1) * cap, :] = jnp.broadcast_to(weight, (cap, 128))

    def send_partial(c, axis, k):
        if axis == 0:
            block = part.at[c, lax.rem(y + k, SIDE), :, :, pl.ds(0, HALF)]
        else:
            block = part.at[c, :, lax.rem(x + k, SIDE), :, pl.ds(HALF, HALF)]
        pltpu.make_async_remote_copy(
            src_ref=block, dst_ref=s1r.at[c, axis, k - 1],
            send_sem=s1s_sem.at[c, axis], recv_sem=s1r_sem.at[c, axis],
            device_id=(along(axis, k), me), device_id_type=MESH,
        ).start()

    def work(c):
        all_of(zrecv.at[c, pl.ds(0, remote)], zr_sem.at[c]).wait()
        load_w(c).wait()
        rows = zrecv[c].astype(F32).reshape(slots, COLS)
        weight = wrep[...]
        weighted = (rows * jnp.concatenate([weight] * (COLS // 128), axis=1)).astype(BF16)
        for k in (1, 2, 3, 0):
            q = lax.rem(y + k, SIDE)
            lhs = hid_t[pl.ds(pl.multiple_of(q * quarter, quarter), quarter), :]
            block = jnp.dot(lhs, weighted, preferred_element_type=F32).astype(BF16)
            part[c, q] = block.reshape(SIDE, share, COLS)
            if k:
                send_partial(c, 0, k)
        for k in (1, 2, 3):
            send_partial(c, 1, k)
        wc = wmat[c]
        out = jnp.dot(hid[...], wc, preferred_element_type=F32) * rows
        total = racc[...]
        for i in range(COLS // 128):
            total = total + out[:, i * 128:(i + 1) * 128]
        racc[...] = total
        gact[...] += lax.dot_general(weighted, wc, (((1,), (1,)), ((), ())), preferred_element_type=F32)

    def sum_first(c):
        for axis in (0, 1):
            all_of(s1r.at[c, axis], s1r_sem.at[c, axis]).wait()
            for k in (1, 2, 3, 0):
                if axis == 0:
                    q = lax.rem(x + k, SIDE)
                    total = part[c, y, q, :, 0:HALF].astype(F32)
                else:
                    q = lax.rem(y + k, SIDE)
                    total = part[c, q, x, :, HALF:COLS].astype(F32)
                top = jnp.abs(total)
                for i in range(SIDE - 1):
                    term = s1r[c, axis, i, q].astype(F32)
                    total = total + term
                    top = jnp.maximum(top, jnp.abs(term))
                s2s[c, axis, q] = total.astype(BF16)
                s2m[c, axis, q] = jnp.max(top.reshape(share // 32, 32, HALF), axis=1)
                if k:
                    peer = (along(1 - axis, k), me)
                    pltpu.make_async_remote_copy(
                        src_ref=s2s.at[c, axis, q], dst_ref=s2r.at[c, axis, k - 1],
                        send_sem=s2s_sem.at[c], recv_sem=s2r_sem.at[c, axis],
                        device_id=peer, device_id_type=MESH,
                    ).start()
                    pltpu.make_async_remote_copy(
                        src_ref=s2m.at[c, axis, q], dst_ref=s2mr.at[c, axis, k - 1],
                        send_sem=m2s_sem.at[c], recv_sem=m2r_sem.at[c, axis],
                        device_id=peer, device_id_type=MESH,
                    ).start()

    def sum_second(c):
        for axis in (0, 1):
            other = y if axis else x
            cols = pl.ds(pl.multiple_of(c * COLS + axis * HALF, HALF), HALF)
            all_of(s2r.at[c, axis], s2r_sem.at[c, axis]).wait()
            all_of(s2mr.at[c, axis], m2r_sem.at[c, axis]).wait()
            total = s2s[c, axis, other].astype(F32)
            top = s2m[c, axis, other]
            for i in range(SIDE - 1):
                total = total + s2r[c, axis, i].astype(F32)
                top = jnp.maximum(top, s2mr[c, axis, i])
            scale = top + TINY
            ws_ref[0, :, cols] = scale
            parts = []
            for b in range(share // 32):
                parts.append(total[b * 32:(b + 1) * 32] / scale[b:b + 1])
            gw_ref[0, :, cols] = jnp.concatenate(parts, axis=0).astype(BF16)

    def step(c, _):
        @pl.when(c + HOPS + RELAYS < chunks)
        def _():
            send_hop(c + HOPS + RELAYS)

        @pl.when(c + RELAYS < chunks)
        def _():
            relay(c + RELAYS)

        work(c)

        @pl.when(c >= LAG1)
        def _():
            sum_first(c - LAG1)

        @pl.when(c >= LAG1 + LAG2)
        def _():
            sum_second(c - LAG1 - LAG2)

        return 0

    lax.fori_loop(0, chunks, step, 0)
    lax.fori_loop(chunks - LAG1, chunks - 1, lambda c, _: (sum_first(c), 0)[1], 0)

    diagonal = c_iota == lax.broadcasted_iota(jnp.int32, (cap, 128), 1).astype(F32)
    for e in range(experts):
        route = jnp.sum(racc[e * cap:(e + 1) * cap, :], axis=1, keepdims=True)
        row = jnp.sum(jnp.where(diagonal, route, 0.0), axis=0, keepdims=True)
        rsend[e] = jnp.broadcast_to(row, (8, 128))
    rrecv[me] = rsend[me]
    for e in zpeers:
        pltpu.make_async_remote_copy(
            src_ref=rsend.at[e], dst_ref=rrecv.at[me], send_sem=rs_sem, recv_sem=rr_sem,
            device_id=(dp, e), device_id_type=MESH,
        ).start()

    def finish(i, _):
        at = pl.ds(pl.multiple_of(i * slab, slab), slab)
        gate = saved[at, :hidden].astype(F32)
        up = saved[at, hidden:].astype(F32)
        sg = jax.nn.sigmoid(gate)
        ga = gact[at, :]
        ggu[0, at, :hidden] = (ga * up * sg * (1.0 + gate * (1.0 - sg))).astype(BF16)
        ggu[0, at, hidden:] = (ga * gate * sg).astype(BF16)
        return 0

    lax.fori_loop(0, slots // slab, finish, 0)

    sum_first(chunks - 1)

    all_of(rrecv.at[pl.ds(0, experts - 1)], rr_sem).wait()
    got = []
    for e in range(experts):
        route = jnp.sum(jnp.where(diagonal, rrecv[e, 0:1, :], 0.0), axis=1, keepdims=True)
        got.append(jnp.sum(picks(rank_s[2, e:e + 1, :]) * route, axis=0, keepdims=True))
    got = jnp.concatenate(got, axis=0)
    for k in range(2):
        gr_ref[k:k + 1, :] = jnp.sum(jnp.where(info_s[k:k + 1, :] == e_iota, got, 0.0), axis=0, keepdims=True)

    lax.fori_loop(chunks - LAG1 - LAG2, chunks, lambda c, _: (sum_second(c), 0)[1], 0)

    all_of(info.at[pl.ds(0, experts - 1)], is_sem).wait()
    all_of(rsend.at[pl.ds(0, experts - 1)], rs_sem).wait()

    def drain(c, _):
        all_of(zrecv.at[c, pl.ds(0, remote)], zs_sem.at[c]).wait()
        all_of(hop.at[c], hs_sem.at[c]).wait()
        all_of(s1r.at[c, 0], s1s_sem.at[c, 0]).wait()
        all_of(s1r.at[c, 1], s1s_sem.at[c, 1]).wait()
        all_of(s2r.at[c], s2s_sem.at[c]).wait()
        all_of(s2mr.at[c], m2s_sem.at[c]).wait()
        return 0

    lax.fori_loop(0, chunks, drain, 0)


def store(*refs):
    sems = refs[-1]
    copies = [pltpu.make_async_copy(refs[i], refs[4 + i], sems.at[i]) for i in range(4)]
    for copy in copies:
        copy.start()
    for copy in copies:
        copy.wait()


def shards(out_grad, route_ids, route_weights, saved_gate_up, down_weight):
    tokens, width = out_grad.shape
    hidden = down_weight.shape[1]
    experts = lax.axis_size("expert")
    slots = saved_gate_up.shape[1]
    cap = slots // experts
    chunks = width // COLS
    share = hidden // SIDE // SIDE
    hbm, vmem = pl.BlockSpec(memory_space=pl.ANY), pl.BlockSpec(memory_space=pltpu.VMEM)
    dma = pltpu.SemaphoreType.DMA
    ggu, gw, ws, gr = pl.pallas_call(
        kernel,
        out_shape=(
            pltpu.VMEM((1, slots, 2 * hidden), BF16),
            pltpu.VMEM((1, share, width), BF16),
            pltpu.VMEM((1, share // 32, width), F32),
            pltpu.VMEM((2, tokens), F32),
        ),
        in_specs=[vmem, vmem, hbm, hbm, hbm],
        out_specs=(vmem,) * 4,
        scratch_shapes=[
            pltpu.VMEM((tokens, width), BF16),
            pltpu.VMEM((slots, 2 * hidden), BF16),
            pltpu.VMEM((chunks, hidden, COLS), BF16),
            pltpu.VMEM((2 * cap, tokens), BF16),
            pltpu.VMEM((2, 7 * cap, tokens), BF16),
            pltpu.VMEM((3, experts, tokens), F32),
            pltpu.VMEM((chunks, 2, tokens, COLS), BF16),
            pltpu.VMEM((chunks, cap, COLS), BF16),
            pltpu.VMEM((chunks, 2, 7, cap, COLS), BF16),
            pltpu.VMEM((chunks, experts, cap, COLS), BF16),
            pltpu.VMEM((8, tokens), F32),
            pltpu.VMEM((experts, 8, tokens), F32),
            pltpu.VMEM((slots, 128), F32),
            pltpu.VMEM((slots, hidden), BF16),
            pltpu.VMEM((hidden, slots), BF16),
            pltpu.VMEM((slots, hidden), F32),
            pltpu.VMEM((slots, 128), F32),
            pltpu.VMEM((chunks, SIDE, SIDE, share, COLS), BF16),
            pltpu.VMEM((chunks, 2, SIDE - 1, SIDE, share, HALF), BF16),
            pltpu.VMEM((chunks, 2, SIDE, share, HALF), BF16),
            pltpu.VMEM((chunks, 2, SIDE, share // 32, HALF), F32),
            pltpu.VMEM((chunks, 2, SIDE - 1, share, HALF), BF16),
            pltpu.VMEM((chunks, 2, SIDE - 1, share // 32, HALF), F32),
            pltpu.VMEM((experts, 8, 128), F32),
            pltpu.VMEM((experts, 8, 128), F32),
            dma((2,)), dma((chunks,)), dma((chunks,)), dma((chunks, 2)), dma((chunks,)), dma((chunks,)), dma, dma((experts,)),
            dma((chunks, 2)), dma((chunks, 2)),
            dma((chunks,)), dma((chunks, 2)), dma((chunks,)), dma((chunks, 2)), dma, dma,
        ],
        compiler_params=pltpu.CompilerParams(
            collective_id=0, has_side_effects=True, vmem_limit_bytes=52 * 2**20
        ),
    )(route_ids.T, route_weights.T, out_grad, saved_gate_up, down_weight)
    ggu, gw, ws, gr = (pltpu.with_memory_space_constraint(o, pltpu.VMEM) for o in (ggu, gw, ws, gr))
    ggu, gw, ws, gr = pl.pallas_call(
        store,
        out_shape=tuple(jax.ShapeDtypeStruct(o.shape, o.dtype) for o in (ggu, gw, ws, gr)),
        in_specs=[vmem] * 4,
        out_specs=(hbm,) * 4,
        scratch_shapes=[dma((4,))],
        compiler_params=pltpu.CompilerParams(vmem_limit_bytes=2**20),
    )(ggu, gw, ws, gr)
    return ggu, gw, ws, gr.T


def solution(mesh):
    in_specs = (
        P(("dp", "expert"), None),
        P(("dp", "expert"), None),
        P(("dp", "expert"), None),
        P(("dp", "expert"), None, None),
        P("expert", None, None),
    )
    out_specs = (
        P(("dp", "expert"), None, None),
        P("expert", "dp", None),
        P("expert", "dp", None),
        P(("dp", "expert"), None),
    )
    return jax.shard_map(shards, mesh=mesh, in_specs=in_specs, out_specs=out_specs, check_vma=False)
```

```python
import functools

import jax
import jax.numpy as jnp
from jax import lax
from jax.experimental import pallas as pl
from jax.experimental.pallas import tpu as pltpu
from jax.sharding import PartitionSpec as P

MESH = pl.DeviceIdType.MESH
F32, BF16 = jnp.float32, jnp.bfloat16
TINY = 1e-06
COLS, HALF = 256, 128
HOPS, RELAYS = 1, 3
LAG1, LAG2 = 2, 2
Z, SIDE = 8, 4


def kernel(
    ids_ref, gate_ref, og_hbm, saved_hbm, w_hbm,
    ggu, gw_ref, ws_ref, gr_ref,
    og, saved, wmat, s_own, s_side, rank_s, hop, zown, zsend, zrecv, info_s, info, wrep, hid, hid_t,
    gact, racc, part, s1r, s2s, s2m, s2r, s2mr, rsend, rrecv,
    in_sem, w_sem, hs_sem, hr_sem, zs_sem, zr_sem, is_sem, ir_sem, s1s_sem, s1r_sem,
    s2s_sem, s2r_sem, m2s_sem, m2r_sem, rs_sem, rr_sem,
):
    chunks = zrecv.shape[0]
    experts, cap = zrecv.shape[1], zrecv.shape[2]
    slots, hidden = hid.shape
    dp, me = lax.axis_index("dp"), lax.axis_index("expert")
    y, x = dp // SIDE, lax.rem(dp, SIDE)
    z, core = me // 2, lax.rem(me, 2)
    quarter = hidden // SIDE
    share = quarter // SIDE

    def expert_at(dz, other):
        return lax.rem(z + dz + Z, Z) * 2 + (1 - core if other else core)

    zpeers = [expert_at(dz, o) for dz in (1, -1, 2, -2, 3, -3, 4, 0) for o in (0, 1) if dz or o]
    near, others = (zpeers[2], zpeers[0]), zpeers[1:2] + zpeers[3:]
    fills = [
        [expert_at(0, 0), expert_at(0, 1), expert_at(d, 0), expert_at(d, 1),
         expert_at(2 * d, 0), expert_at(2 * d, 1), expert_at(3 * d, d < 0)]
        for d in (1, -1)
    ]
    remote = experts - 3

    def along(axis, step):
        return lax.rem(y + step * (1 - axis), SIDE) * SIDE + lax.rem(x + step * axis, SIDE)

    load_og = pltpu.make_async_copy(og_hbm, og, in_sem.at[0])
    load_saved = pltpu.make_async_copy(saved_hbm.at[0], saved, in_sem.at[1])

    def load_w(c):
        cols = pl.ds(pl.multiple_of(c * COLS, COLS), COLS)
        return pltpu.make_async_copy(w_hbm.at[0, :, cols], wmat.at[c], w_sem.at[c])

    load_og.start()
    load_saved.start()

    barrier = pltpu.get_barrier_semaphore()
    for e in zpeers:
        pl.semaphore_signal(barrier, inc=1, device_id=(dp, e), device_id_type=MESH)
    for step in (1, 2, 3):
        for axis in (0, 1):
            pl.semaphore_signal(barrier, inc=1, device_id=(along(axis, step), me), device_id_type=MESH)

    tokens = ids_ref.shape[1]
    earlier = (
        lax.broadcasted_iota(jnp.int32, (tokens, tokens), 0)
        < lax.broadcasted_iota(jnp.int32, (tokens, tokens), 1)
    ).astype(F32).astype(BF16)
    c_iota = lax.broadcasted_iota(jnp.int32, (cap, tokens), 0).astype(F32)
    e_iota = lax.broadcasted_iota(jnp.int32, (experts, tokens), 0).astype(F32)
    info_s[...] = jnp.zeros_like(info_s)
    info_s[0:2, :] = ids_ref[...].astype(F32)
    info_s[2:4, :] = gate_ref[...].astype(F32)
    info[me] = info_s[...]

    def ranks(named):
        rank = jnp.dot(named.astype(F32).astype(BF16), earlier, preferred_element_type=F32)
        return jnp.where(named, rank, -1.0)

    def picks(rank_row):
        return jnp.where(rank_row == c_iota, 1.0, 0.0)

    def rank_of(i, source):
        first, second = info[source, 0:1, :], info[source, 1:2, :]
        rank_s[i] = ranks((first == e_iota) | (second == e_iota))

    rank_of(2, me)
    s_own[...] = jnp.concatenate([picks(rank_s[2, pl.ds(e, 1), :]) for e in fills[0][:2]], axis=0).astype(BF16)

    pl.semaphore_wait(barrier, len(zpeers) + 6)

    def send_hop(c):
        cols = pl.ds(pl.multiple_of(c * COLS, COLS), COLS)
        for side in (0, 1):
            pltpu.make_async_remote_copy(
                src_ref=og_hbm.at[:, cols], dst_ref=hop.at[c, side],
                send_sem=hs_sem.at[c], recv_sem=hr_sem.at[c, side],
                device_id=(dp, near[1 - side]), device_id_type=MESH,
            ).start()

    def send_info(e):
        pltpu.make_async_remote_copy(
            src_ref=info_s, dst_ref=info.at[me], send_sem=is_sem, recv_sem=ir_sem.at[me],
            device_id=(dp, e), device_id_type=MESH,
        ).start()

    def wait_info(e):
        pltpu.make_async_copy(info.at[e], info.at[e], ir_sem.at[e]).wait()

    send_info(near[0])
    send_info(near[1])
    lax.fori_loop(0, HOPS + RELAYS, lambda c, _: (send_hop(c), 0)[1], 0)
    for e in others:
        send_info(e)
    for side in (0, 1):
        wait_info(near[side])
        rank_of(side, near[side])
        s_side[side] = jnp.concatenate([picks(rank_s[side, pl.ds(e, 1), :]) for e in fills[side]], axis=0).astype(BF16)
    load_og.wait()

    def send_rows(block, c, source, target):
        pltpu.make_async_remote_copy(
            src_ref=block, dst_ref=zrecv.at[c, source],
            send_sem=zs_sem.at[c], recv_sem=zr_sem.at[c],
            device_id=(dp, target), device_id_type=MESH,
        ).start()

    def relay(c):
        cols = pl.ds(pl.multiple_of(c * COLS, COLS), COLS)
        block = jnp.dot(s_own[...], og[:, cols], preferred_element_type=F32)
        block = block.reshape(2, cap, COLS).astype(BF16)
        zrecv[c, me] = block[0]
        zown[c] = block[1]
        send_rows(zown.at[c], c, me, fills[0][1])
        for side in (0, 1):
            pltpu.make_async_copy(hop.at[c, side], hop.at[c, side], hr_sem.at[c, side]).wait()
            block = jnp.dot(s_side[side], hop[c, side], preferred_element_type=F32)
            block = block.reshape(7, cap, COLS).astype(BF16)
            zrecv[c, near[side]] = block[0]
            zsend[c, side] = block
            for i in (6, 4, 5, 2, 3, 1):
                send_rows(zsend.at[c, side, i], c, near[side], fills[side][i])
        load_w(c).start()

    lax.fori_loop(0, RELAYS, lambda c, _: (relay(c), 0)[1], 0)

    load_saved.wait()
    slab = 128

    def activate(i, _):
        at = pl.ds(pl.multiple_of(i * slab, slab), slab)
        gate = saved[at, :hidden].astype(F32)
        up = saved[at, hidden:].astype(F32)
        act = gate * jax.nn.sigmoid(gate) * up
        hid[at, :] = act.astype(BF16)
        hid_t[:, at] = act.T.astype(BF16)
        return 0

    lax.fori_loop(0, slots // slab, activate, 0)
    gact[...] = jnp.zeros_like(gact)
    racc[...] = jnp.zeros_like(racc)

    def all_of(ref, sem):
        return pltpu.make_async_copy(ref, ref, sem)

    for e in others:
        wait_info(e)
    first = jnp.concatenate([info[e, 0:1, :] for e in range(experts)], axis=0)
    second = jnp.concatenate([info[e, 1:2, :] for e in range(experts)], axis=0)
    mine = me.astype(F32)
    rank = ranks((first == mine) | (second == mine))
    for e in range(experts):
        gates = jnp.where(first[e:e + 1] == mine, info[e, 2:3, :], info[e, 3:4, :])
        weight = jnp.sum(picks(rank[e:e + 1]) * gates, axis=1, keepdims=True)
        wrep[e * cap:(e + 1) * cap, :] = jnp.broadcast_to(weight, (cap, 128))

    def send_partial(c, axis, k):
        if axis == 0:
            block = part.at[c, lax.rem(y + k, SIDE), :, :, pl.ds(0, HALF)]
        else:
            block = part.at[c, :, lax.rem(x + k, SIDE), :, pl.ds(HALF, HALF)]
        pltpu.make_async_remote_copy(
            src_ref=block, dst_ref=s1r.at[c, axis, k - 1],
            send_sem=s1s_sem.at[c, axis], recv_sem=s1r_sem.at[c, axis],
            device_id=(along(axis, k), me), device_id_type=MESH,
        ).start()

    def work(c):
        all_of(zrecv.at[c, pl.ds(0, remote)], zr_sem.at[c]).wait()
        load_w(c).wait()
        rows = zrecv[c].astype(F32).reshape(slots, COLS)
        weight = wrep[...]
        weighted = (rows * jnp.concatenate([weight] * (COLS // 128), axis=1)).astype(BF16)
        for k in (1, 2, 3, 0):
            q = lax.rem(y + k, SIDE)
            lhs = hid_t[pl.ds(pl.multiple_of(q * quarter, quarter), quarter), :]
            block = jnp.dot(lhs, weighted, preferred_element_type=F32).astype(BF16)
            part[c, q] = block.reshape(SIDE, share, COLS)
            if k:
                send_partial(c, 0, k)
        for k in (1, 2, 3):
            send_partial(c, 1, k)
        wc = wmat[c]
        out = jnp.dot(hid[...], wc, preferred_element_type=F32) * rows
        total = racc[...]
        for i in range(COLS // 128):
            total = total + out[:, i * 128:(i + 1) * 128]
        racc[...] = total
        gact[...] += lax.dot_general(weighted, wc, (((1,), (1,)), ((), ())), preferred_element_type=F32)

    def sum_first(c):
        for axis in (0, 1):
            all_of(s1r.at[c, axis], s1r_sem.at[c, axis]).wait()
            for k in (1, 2, 3, 0):
                if axis == 0:
                    q = lax.rem(x + k, SIDE)
                    total = part[c, y, q, :, 0:HALF].astype(F32)
                else:
                    q = lax.rem(y + k, SIDE)
                    total = part[c, q, x, :, HALF:COLS].astype(F32)
                top = jnp.abs(total)
                for i in range(SIDE - 1):
                    term = s1r[c, axis, i, q].astype(F32)
                    total = total + term
                    top = jnp.maximum(top, jnp.abs(term))
                s2s[c, axis, q] = total.astype(BF16)
                s2m[c, axis, q] = jnp.max(top.reshape(share // 32, 32, HALF), axis=1)
                if k:
                    peer = (along(1 - axis, k), me)
                    pltpu.make_async_remote_copy(
                        src_ref=s2s.at[c, axis, q], dst_ref=s2r.at[c, axis, k - 1],
                        send_sem=s2s_sem.at[c], recv_sem=s2r_sem.at[c, axis],
                        device_id=peer, device_id_type=MESH,
                    ).start()
                    pltpu.make_async_remote_copy(
                        src_ref=s2m.at[c, axis, q], dst_ref=s2mr.at[c, axis, k - 1],
                        send_sem=m2s_sem.at[c], recv_sem=m2r_sem.at[c, axis],
                        device_id=peer, device_id_type=MESH,
                    ).start()

    def sum_second(c):
        for axis in (0, 1):
            other = y if axis else x
            cols = pl.ds(pl.multiple_of(c * COLS + axis * HALF, HALF), HALF)
            all_of(s2r.at[c, axis], s2r_sem.at[c, axis]).wait()
            all_of(s2mr.at[c, axis], m2r_sem.at[c, axis]).wait()
            total = s2s[c, axis, other].astype(F32)
            top = s2m[c, axis, other]
            for i in range(SIDE - 1):
                total = total + s2r[c, axis, i].astype(F32)
                top = jnp.maximum(top, s2mr[c, axis, i])
            scale = top + TINY
            ws_ref[0, :, cols] = scale
            parts = []
            for b in range(share // 32):
                parts.append(total[b * 32:(b + 1) * 32] / scale[b:b + 1])
            gw_ref[0, :, cols] = jnp.concatenate(parts, axis=0).astype(BF16)

    def step(c, _):
        @pl.when(c + HOPS + RELAYS < chunks)
        def _():
            send_hop(c + HOPS + RELAYS)


        @pl.when(c >= LAG1)
        def _():
            sum_first(c - LAG1)

        work(c)

        @pl.when(c + RELAYS < chunks)
        def _():
            relay(c + RELAYS)

        @pl.when(c >= LAG1 + LAG2)
        def _():
            sum_second(c - LAG1 - LAG2)

        return 0

    lax.fori_loop(0, chunks, step, 0)
    lax.fori_loop(chunks - LAG1, chunks - 1, lambda c, _: (sum_first(c), 0)[1], 0)

    diagonal = c_iota == lax.broadcasted_iota(jnp.int32, (cap, 128), 1).astype(F32)
    for e in range(experts):
        route = jnp.sum(racc[e * cap:(e + 1) * cap, :], axis=1, keepdims=True)
        row = jnp.sum(jnp.where(diagonal, route, 0.0), axis=0, keepdims=True)
        rsend[e] = jnp.broadcast_to(row, (8, 128))
    rrecv[me] = rsend[me]
    for e in zpeers:
        pltpu.make_async_remote_copy(
            src_ref=rsend.at[e], dst_ref=rrecv.at[me], send_sem=rs_sem, recv_sem=rr_sem,
            device_id=(dp, e), device_id_type=MESH,
        ).start()

    def finish(i, _):
        at = pl.ds(pl.multiple_of(i * slab, slab), slab)
        gate = saved[at, :hidden].astype(F32)
        up = saved[at, hidden:].astype(F32)
        sg = jax.nn.sigmoid(gate)
        ga = gact[at, :]
        ggu[0, at, :hidden] = (ga * up * sg * (1.0 + gate * (1.0 - sg))).astype(BF16)
        ggu[0, at, hidden:] = (ga * gate * sg).astype(BF16)
        return 0

    lax.fori_loop(0, slots // slab, finish, 0)

    sum_first(chunks - 1)

    all_of(rrecv.at[pl.ds(0, experts - 1)], rr_sem).wait()
    got = []
    for e in range(experts):
        route = jnp.sum(jnp.where(diagonal, rrecv[e, 0:1, :], 0.0), axis=1, keepdims=True)
        got.append(jnp.sum(picks(rank_s[2, e:e + 1, :]) * route, axis=0, keepdims=True))
    got = jnp.concatenate(got, axis=0)
    for k in range(2):
        gr_ref[k:k + 1, :] = jnp.sum(jnp.where(info_s[k:k + 1, :] == e_iota, got, 0.0), axis=0, keepdims=True)

    lax.fori_loop(chunks - LAG1 - LAG2, chunks, lambda c, _: (sum_second(c), 0)[1], 0)

    all_of(info.at[pl.ds(0, experts - 1)], is_sem).wait()
    all_of(rsend.at[pl.ds(0, experts - 1)], rs_sem).wait()

    def drain(c, _):
        all_of(zrecv.at[c, pl.ds(0, remote)], zs_sem.at[c]).wait()
        all_of(hop.at[c], hs_sem.at[c]).wait()
        all_of(s1r.at[c, 0], s1s_sem.at[c, 0]).wait()
        all_of(s1r.at[c, 1], s1s_sem.at[c, 1]).wait()
        all_of(s2r.at[c], s2s_sem.at[c]).wait()
        all_of(s2mr.at[c], m2s_sem.at[c]).wait()
        return 0

    lax.fori_loop(0, chunks, drain, 0)


def store(*refs):
    sems = refs[-1]
    copies = [pltpu.make_async_copy(refs[i], refs[4 + i], sems.at[i]) for i in range(4)]
    for copy in copies:
        copy.start()
    for copy in copies:
        copy.wait()


def shards(out_grad, route_ids, route_weights, saved_gate_up, down_weight):
    tokens, width = out_grad.shape
    hidden = down_weight.shape[1]
    experts = lax.axis_size("expert")
    slots = saved_gate_up.shape[1]
    cap = slots // experts
    chunks = width // COLS
    share = hidden // SIDE // SIDE
    hbm, vmem = pl.BlockSpec(memory_space=pl.ANY), pl.BlockSpec(memory_space=pltpu.VMEM)
    dma = pltpu.SemaphoreType.DMA
    ggu, gw, ws, gr = pl.pallas_call(
        kernel,
        out_shape=(
            pltpu.VMEM((1, slots, 2 * hidden), BF16),
            pltpu.VMEM((1, share, width), BF16),
            pltpu.VMEM((1, share // 32, width), F32),
            pltpu.VMEM((2, tokens), F32),
        ),
        in_specs=[vmem, vmem, hbm, hbm, hbm],
        out_specs=(vmem,) * 4,
        scratch_shapes=[
            pltpu.VMEM((tokens, width), BF16),
            pltpu.VMEM((slots, 2 * hidden), BF16),
            pltpu.VMEM((chunks, hidden, COLS), BF16),
            pltpu.VMEM((2 * cap, tokens), BF16),
            pltpu.VMEM((2, 7 * cap, tokens), BF16),
            pltpu.VMEM((3, experts, tokens), F32),
            pltpu.VMEM((chunks, 2, tokens, COLS), BF16),
            pltpu.VMEM((chunks, cap, COLS), BF16),
            pltpu.VMEM((chunks, 2, 7, cap, COLS), BF16),
            pltpu.VMEM((chunks, experts, cap, COLS), BF16),
            pltpu.VMEM((8, tokens), F32),
            pltpu.VMEM((experts, 8, tokens), F32),
            pltpu.VMEM((slots, 128), F32),
            pltpu.VMEM((slots, hidden), BF16),
            pltpu.VMEM((hidden, slots), BF16),
            pltpu.VMEM((slots, hidden), F32),
            pltpu.VMEM((slots, 128), F32),
            pltpu.VMEM((chunks, SIDE, SIDE, share, COLS), BF16),
            pltpu.VMEM((chunks, 2, SIDE - 1, SIDE, share, HALF), BF16),
            pltpu.VMEM((chunks, 2, SIDE, share, HALF), BF16),
            pltpu.VMEM((chunks, 2, SIDE, share // 32, HALF), F32),
            pltpu.VMEM((chunks, 2, SIDE - 1, share, HALF), BF16),
            pltpu.VMEM((chunks, 2, SIDE - 1, share // 32, HALF), F32),
            pltpu.VMEM((experts, 8, 128), F32),
            pltpu.VMEM((experts, 8, 128), F32),
            dma((2,)), dma((chunks,)), dma((chunks,)), dma((chunks, 2)), dma((chunks,)), dma((chunks,)), dma, dma((experts,)),
            dma((chunks, 2)), dma((chunks, 2)),
            dma((chunks,)), dma((chunks, 2)), dma((chunks,)), dma((chunks, 2)), dma, dma,
        ],
        compiler_params=pltpu.CompilerParams(
            collective_id=0, has_side_effects=True, vmem_limit_bytes=52 * 2**20
        ),
    )(route_ids.T, route_weights.T, out_grad, saved_gate_up, down_weight)
    ggu, gw, ws, gr = (pltpu.with_memory_space_constraint(o, pltpu.VMEM) for o in (ggu, gw, ws, gr))
    ggu, gw, ws, gr = pl.pallas_call(
        store,
        out_shape=tuple(jax.ShapeDtypeStruct(o.shape, o.dtype) for o in (ggu, gw, ws, gr)),
        in_specs=[vmem] * 4,
        out_specs=(hbm,) * 4,
        scratch_shapes=[dma((4,))],
        compiler_params=pltpu.CompilerParams(vmem_limit_bytes=2**20),
    )(ggu, gw, ws, gr)
    return ggu, gw, ws, gr.T


def solution(mesh):
    in_specs = (
        P(("dp", "expert"), None),
        P(("dp", "expert"), None),
        P(("dp", "expert"), None),
        P(("dp", "expert"), None, None),
        P("expert", None, None),
    )
    out_specs = (
        P(("dp", "expert"), None, None),
        P("expert", "dp", None),
        P("expert", "dp", None),
        P(("dp", "expert"), None),
    )
    return jax.shard_map(shards, mesh=mesh, in_specs=in_specs, out_specs=out_specs, check_vma=False)
```

```python
import functools

import jax
import jax.numpy as jnp
from jax import lax
from jax.experimental import pallas as pl
from jax.experimental.pallas import tpu as pltpu
from jax.sharding import PartitionSpec as P

MESH = pl.DeviceIdType.MESH
F32, BF16 = jnp.float32, jnp.bfloat16
TINY = 1e-06
COLS, HALF = 256, 128
HOPS, RELAYS = 1, 3
LAG1, LAG2 = 2, 2
Z, SIDE = 8, 4


def kernel(
    ids_ref, gate_ref, og_hbm, saved_hbm, w_hbm,
    ggu, gw_ref, ws_ref, gr_ref,
    og, saved, wmat, s_own, s_side, rank_s, hop, zown, zsend, zrecv, info_s, info, wrep, hid, hid_t,
    gact, racc, part, s1r, s2s, s2m, s2r, s2mr, rsend, rrecv,
    in_sem, w_sem, hs_sem, hr_sem, zs_sem, zr_sem, is_sem, ir_sem, s1s_sem, s1r_sem,
    s2s_sem, s2r_sem, m2s_sem, m2r_sem, rs_sem, rr_sem,
):
    chunks = zrecv.shape[0]
    experts, cap = zrecv.shape[1], zrecv.shape[2]
    slots, hidden = hid.shape
    dp, me = lax.axis_index("dp"), lax.axis_index("expert")
    y, x = dp // SIDE, lax.rem(dp, SIDE)
    z, core = me // 2, lax.rem(me, 2)
    quarter = hidden // SIDE
    share = quarter // SIDE

    def expert_at(dz, other):
        return lax.rem(z + dz + Z, Z) * 2 + (1 - core if other else core)

    zpeers = [expert_at(dz, o) for dz in (1, -1, 2, -2, 3, -3, 4, 0) for o in (0, 1) if dz or o]
    near, others = (zpeers[2], zpeers[0]), zpeers[1:2] + zpeers[3:]
    fills = [
        [expert_at(0, 0), expert_at(0, 1), expert_at(d, 0), expert_at(d, 1),
         expert_at(2 * d, 0), expert_at(2 * d, 1), expert_at(3 * d, d < 0)]
        for d in (1, -1)
    ]
    remote = experts - 3

    def along(axis, step):
        return lax.rem(y + step * (1 - axis), SIDE) * SIDE + lax.rem(x + step * axis, SIDE)

    load_og = pltpu.make_async_copy(og_hbm, og, in_sem.at[0])
    load_saved = pltpu.make_async_copy(saved_hbm.at[0], saved, in_sem.at[1])

    def load_w(c):
        cols = pl.ds(pl.multiple_of(c * COLS, COLS), COLS)
        return pltpu.make_async_copy(w_hbm.at[0, :, cols], wmat.at[c], w_sem.at[c])

    load_og.start()
    load_saved.start()

    barrier = pltpu.get_barrier_semaphore()
    for e in zpeers:
        pl.semaphore_signal(barrier, inc=1, device_id=(dp, e), device_id_type=MESH)
    for step in (1, 2, 3):
        for axis in (0, 1):
            pl.semaphore_signal(barrier, inc=1, device_id=(along(axis, step), me), device_id_type=MESH)

    tokens = ids_ref.shape[1]
    earlier = (
        lax.broadcasted_iota(jnp.int32, (tokens, tokens), 0)
        < lax.broadcasted_iota(jnp.int32, (tokens, tokens), 1)
    ).astype(F32).astype(BF16)
    c_iota = lax.broadcasted_iota(jnp.int32, (cap, tokens), 0).astype(F32)
    e_iota = lax.broadcasted_iota(jnp.int32, (experts, tokens), 0).astype(F32)
    info_s[...] = jnp.zeros_like(info_s)
    info_s[0:2, :] = ids_ref[...].astype(F32)
    info_s[2:4, :] = gate_ref[...].astype(F32)
    info[me] = info_s[...]

    def ranks(named):
        rank = jnp.dot(named.astype(F32).astype(BF16), earlier, preferred_element_type=F32)
        return jnp.where(named, rank, -1.0)

    def picks(rank_row):
        return jnp.where(rank_row == c_iota, 1.0, 0.0)

    def rank_of(i, source):
        first, second = info[source, 0:1, :], info[source, 1:2, :]
        rank_s[i] = ranks((first == e_iota) | (second == e_iota))

    rank_of(2, me)
    s_own[...] = jnp.concatenate([picks(rank_s[2, pl.ds(e, 1), :]) for e in fills[0][:2]], axis=0).astype(BF16)

    load_og.wait()
    pl.semaphore_wait(barrier, len(zpeers) + 6)

    def send_hop(c):
        cols = pl.ds(pl.multiple_of(c * COLS, COLS), COLS)
        for side in (0, 1):
            pltpu.make_async_remote_copy(
                src_ref=og.at[:, cols], dst_ref=hop.at[c, side],
                send_sem=hs_sem.at[c], recv_sem=hr_sem.at[c, side],
                device_id=(dp, near[1 - side]), device_id_type=MESH,
            ).start()

    def send_info(e):
        pltpu.make_async_remote_copy(
            src_ref=info_s, dst_ref=info.at[me], send_sem=is_sem, recv_sem=ir_sem.at[me],
            device_id=(dp, e), device_id_type=MESH,
        ).start()

    def wait_info(e):
        pltpu.make_async_copy(info.at[e], info.at[e], ir_sem.at[e]).wait()

    send_info(near[0])
    send_info(near[1])
    lax.fori_loop(0, HOPS + RELAYS, lambda c, _: (send_hop(c), 0)[1], 0)
    for e in others:
        send_info(e)
    for side in (0, 1):
        wait_info(near[side])
        rank_of(side, near[side])
        s_side[side] = jnp.concatenate([picks(rank_s[side, pl.ds(e, 1), :]) for e in fills[side]], axis=0).astype(BF16)

    def send_rows(block, c, source, target):
        pltpu.make_async_remote_copy(
            src_ref=block, dst_ref=zrecv.at[c, source],
            send_sem=zs_sem.at[c], recv_sem=zr_sem.at[c],
            device_id=(dp, target), device_id_type=MESH,
        ).start()

    def relay(c):
        cols = pl.ds(pl.multiple_of(c * COLS, COLS), COLS)
        block = jnp.dot(s_own[...], og[:, cols], preferred_element_type=F32)
        block = block.reshape(2, cap, COLS).astype(BF16)
        zrecv[c, me] = block[0]
        zown[c] = block[1]
        send_rows(zown.at[c], c, me, fills[0][1])
        for side in (0, 1):
            pltpu.make_async_copy(hop.at[c, side], hop.at[c, side], hr_sem.at[c, side]).wait()
            block = jnp.dot(s_side[side], hop[c, side], preferred_element_type=F32)
            block = block.reshape(7, cap, COLS).astype(BF16)
            zrecv[c, near[side]] = block[0]
            zsend[c, side] = block
            for i in (1, 2, 3, 4, 5, 6):
                send_rows(zsend.at[c, side, i], c, near[side], fills[side][i])
        load_w(c).start()

    lax.fori_loop(0, RELAYS, lambda c, _: (relay(c), 0)[1], 0)

    load_saved.wait()
    slab = 128

    def activate(i, _):
        at = pl.ds(pl.multiple_of(i * slab, slab), slab)
        gate = saved[at, :hidden].astype(F32)
        up = saved[at, hidden:].astype(F32)
        act = gate * jax.nn.sigmoid(gate) * up
        hid[at, :] = act.astype(BF16)
        hid_t[:, at] = act.T.astype(BF16)
        return 0

    lax.fori_loop(0, slots // slab, activate, 0)
    gact[...] = jnp.zeros_like(gact)
    racc[...] = jnp.zeros_like(racc)

    def all_of(ref, sem):
        return pltpu.make_async_copy(ref, ref, sem)

    for e in others:
        wait_info(e)
    first = jnp.concatenate([info[e, 0:1, :] for e in range(experts)], axis=0)
    second = jnp.concatenate([info[e, 1:2, :] for e in range(experts)], axis=0)
    mine = me.astype(F32)
    rank = ranks((first == mine) | (second == mine))
    for e in range(experts):
        gates = jnp.where(first[e:e + 1] == mine, info[e, 2:3, :], info[e, 3:4, :])
        weight = jnp.sum(picks(rank[e:e + 1]) * gates, axis=1, keepdims=True)
        wrep[e * cap:(e + 1) * cap, :] = jnp.broadcast_to(weight, (cap, 128))

    def send_partial(c, axis, k):
        if axis == 0:
            block = part.at[c, lax.rem(y + k, SIDE), :, :, pl.ds(0, HALF)]
        else:
            block = part.at[c, :, lax.rem(x + k, SIDE), :, pl.ds(HALF, HALF)]
        pltpu.make_async_remote_copy(
            src_ref=block, dst_ref=s1r.at[c, axis, k - 1],
            send_sem=s1s_sem.at[c, axis], recv_sem=s1r_sem.at[c, axis],
            device_id=(along(axis, k), me), device_id_type=MESH,
        ).start()

    def work(c):
        all_of(zrecv.at[c, pl.ds(0, remote)], zr_sem.at[c]).wait()
        load_w(c).wait()
        rows = zrecv[c].astype(F32).reshape(slots, COLS)
        weight = wrep[...]
        weighted = (rows * jnp.concatenate([weight] * (COLS // 128), axis=1)).astype(BF16)
        for k in (1, 2, 3, 0):
            q = lax.rem(y + k, SIDE)
            lhs = hid_t[pl.ds(pl.multiple_of(q * quarter, quarter), quarter), :]
            block = jnp.dot(lhs, weighted, preferred_element_type=F32).astype(BF16)
            part[c, q] = block.reshape(SIDE, share, COLS)
            if k:
                send_partial(c, 0, k)
        for k in (1, 2, 3):
            send_partial(c, 1, k)
        wc = wmat[c]
        out = jnp.dot(hid[...], wc, preferred_element_type=F32) * rows
        total = racc[...]
        for i in range(COLS // 128):
            total = total + out[:, i * 128:(i + 1) * 128]
        racc[...] = total
        gact[...] += lax.dot_general(weighted, wc, (((1,), (1,)), ((), ())), preferred_element_type=F32)

    def sum_first(c):
        for axis in (0, 1):
            all_of(s1r.at[c, axis], s1r_sem.at[c, axis]).wait()
            for k in (1, 2, 3, 0):
                if axis == 0:
                    q = lax.rem(x + k, SIDE)
                    total = part[c, y, q, :, 0:HALF].astype(F32)
                else:
                    q = lax.rem(y + k, SIDE)
                    total = part[c, q, x, :, HALF:COLS].astype(F32)
                top = jnp.abs(total)
                for i in range(SIDE - 1):
                    term = s1r[c, axis, i, q].astype(F32)
                    total = total + term
                    top = jnp.maximum(top, jnp.abs(term))
                s2s[c, axis, q] = total.astype(BF16)
                s2m[c, axis, q] = jnp.max(top.reshape(share // 32, 32, HALF), axis=1)
                if k:
                    peer = (along(1 - axis, k), me)
                    pltpu.make_async_remote_copy(
                        src_ref=s2s.at[c, axis, q], dst_ref=s2r.at[c, axis, k - 1],
                        send_sem=s2s_sem.at[c], recv_sem=s2r_sem.at[c, axis],
                        device_id=peer, device_id_type=MESH,
                    ).start()
                    pltpu.make_async_remote_copy(
                        src_ref=s2m.at[c, axis, q], dst_ref=s2mr.at[c, axis, k - 1],
                        send_sem=m2s_sem.at[c], recv_sem=m2r_sem.at[c, axis],
                        device_id=peer, device_id_type=MESH,
                    ).start()

    def sum_second(c):
        for axis in (0, 1):
            other = y if axis else x
            cols = pl.ds(pl.multiple_of(c * COLS + axis * HALF, HALF), HALF)
            all_of(s2r.at[c, axis], s2r_sem.at[c, axis]).wait()
            all_of(s2mr.at[c, axis], m2r_sem.at[c, axis]).wait()
            total = s2s[c, axis, other].astype(F32)
            top = s2m[c, axis, other]
            for i in range(SIDE - 1):
                total = total + s2r[c, axis, i].astype(F32)
                top = jnp.maximum(top, s2mr[c, axis, i])
            scale = top + TINY
            ws_ref[0, :, cols] = scale
            parts = []
            for b in range(share // 32):
                parts.append(total[b * 32:(b + 1) * 32] / scale[b:b + 1])
            gw_ref[0, :, cols] = jnp.concatenate(parts, axis=0).astype(BF16)

    def step(c, _):
        @pl.when(c + HOPS + RELAYS < chunks)
        def _():
            send_hop(c + HOPS + RELAYS)


        @pl.when(c >= LAG1)
        def _():
            sum_first(c - LAG1)

        work(c)

        @pl.when(c + RELAYS < chunks)
        def _():
            relay(c + RELAYS)

        @pl.when(c >= LAG1 + LAG2)
        def _():
            sum_second(c - LAG1 - LAG2)

        return 0

    lax.fori_loop(0, chunks, step, 0)
    lax.fori_loop(chunks - LAG1, chunks - 1, lambda c, _: (sum_first(c), 0)[1], 0)

    diagonal = c_iota == lax.broadcasted_iota(jnp.int32, (cap, 128), 1).astype(F32)
    for e in range(experts):
        route = jnp.sum(racc[e * cap:(e + 1) * cap, :], axis=1, keepdims=True)
        row = jnp.sum(jnp.where(diagonal, route, 0.0), axis=0, keepdims=True)
        rsend[e] = jnp.broadcast_to(row, (8, 128))
    rrecv[me] = rsend[me]
    for e in zpeers:
        pltpu.make_async_remote_copy(
            src_ref=rsend.at[e], dst_ref=rrecv.at[me], send_sem=rs_sem, recv_sem=rr_sem,
            device_id=(dp, e), device_id_type=MESH,
        ).start()

    def finish(i, _):
        at = pl.ds(pl.multiple_of(i * slab, slab), slab)
        gate = saved[at, :hidden].astype(F32)
        up = saved[at, hidden:].astype(F32)
        sg = jax.nn.sigmoid(gate)
        ga = gact[at, :]
        ggu[0, at, :hidden] = (ga * up * sg * (1.0 + gate * (1.0 - sg))).astype(BF16)
        ggu[0, at, hidden:] = (ga * gate * sg).astype(BF16)
        return 0

    lax.fori_loop(0, slots // slab, finish, 0)

    sum_first(chunks - 1)

    all_of(rrecv.at[pl.ds(0, experts - 1)], rr_sem).wait()
    got = []
    for e in range(experts):
        route = jnp.sum(jnp.where(diagonal, rrecv[e, 0:1, :], 0.0), axis=1, keepdims=True)
        got.append(jnp.sum(picks(rank_s[2, e:e + 1, :]) * route, axis=0, keepdims=True))
    got = jnp.concatenate(got, axis=0)
    for k in range(2):
        gr_ref[k:k + 1, :] = jnp.sum(jnp.where(info_s[k:k + 1, :] == e_iota, got, 0.0), axis=0, keepdims=True)

    lax.fori_loop(chunks - LAG1 - LAG2, chunks, lambda c, _: (sum_second(c), 0)[1], 0)

    all_of(info.at[pl.ds(0, experts - 1)], is_sem).wait()
    all_of(rsend.at[pl.ds(0, experts - 1)], rs_sem).wait()

    def drain(c, _):
        all_of(zrecv.at[c, pl.ds(0, remote)], zs_sem.at[c]).wait()
        all_of(hop.at[c], hs_sem.at[c]).wait()
        all_of(s1r.at[c, 0], s1s_sem.at[c, 0]).wait()
        all_of(s1r.at[c, 1], s1s_sem.at[c, 1]).wait()
        all_of(s2r.at[c], s2s_sem.at[c]).wait()
        all_of(s2mr.at[c], m2s_sem.at[c]).wait()
        return 0

    lax.fori_loop(0, chunks, drain, 0)


def store(*refs):
    sems = refs[-1]
    copies = [pltpu.make_async_copy(refs[i], refs[4 + i], sems.at[i]) for i in range(4)]
    for copy in copies:
        copy.start()
    for copy in copies:
        copy.wait()


def shards(out_grad, route_ids, route_weights, saved_gate_up, down_weight):
    tokens, width = out_grad.shape
    hidden = down_weight.shape[1]
    experts = lax.axis_size("expert")
    slots = saved_gate_up.shape[1]
    cap = slots // experts
    chunks = width // COLS
    share = hidden // SIDE // SIDE
    hbm, vmem = pl.BlockSpec(memory_space=pl.ANY), pl.BlockSpec(memory_space=pltpu.VMEM)
    dma = pltpu.SemaphoreType.DMA
    ggu, gw, ws, gr = pl.pallas_call(
        kernel,
        out_shape=(
            pltpu.VMEM((1, slots, 2 * hidden), BF16),
            pltpu.VMEM((1, share, width), BF16),
            pltpu.VMEM((1, share // 32, width), F32),
            pltpu.VMEM((2, tokens), F32),
        ),
        in_specs=[vmem, vmem, hbm, hbm, hbm],
        out_specs=(vmem,) * 4,
        scratch_shapes=[
            pltpu.VMEM((tokens, width), BF16),
            pltpu.VMEM((slots, 2 * hidden), BF16),
            pltpu.VMEM((chunks, hidden, COLS), BF16),
            pltpu.VMEM((2 * cap, tokens), BF16),
            pltpu.VMEM((2, 7 * cap, tokens), BF16),
            pltpu.VMEM((3, experts, tokens), F32),
            pltpu.VMEM((chunks, 2, tokens, COLS), BF16),
            pltpu.VMEM((chunks, cap, COLS), BF16),
            pltpu.VMEM((chunks, 2, 7, cap, COLS), BF16),
            pltpu.VMEM((chunks, experts, cap, COLS), BF16),
            pltpu.VMEM((8, tokens), F32),
            pltpu.VMEM((experts, 8, tokens), F32),
            pltpu.VMEM((slots, 128), F32),
            pltpu.VMEM((slots, hidden), BF16),
            pltpu.VMEM((hidden, slots), BF16),
            pltpu.VMEM((slots, hidden), F32),
            pltpu.VMEM((slots, 128), F32),
            pltpu.VMEM((chunks, SIDE, SIDE, share, COLS), BF16),
            pltpu.VMEM((chunks, 2, SIDE - 1, SIDE, share, HALF), BF16),
            pltpu.VMEM((chunks, 2, SIDE, share, HALF), BF16),
            pltpu.VMEM((chunks, 2, SIDE, share // 32, HALF), F32),
            pltpu.VMEM((chunks, 2, SIDE - 1, share, HALF), BF16),
            pltpu.VMEM((chunks, 2, SIDE - 1, share // 32, HALF), F32),
            pltpu.VMEM((experts, 8, 128), F32),
            pltpu.VMEM((experts, 8, 128), F32),
            dma((2,)), dma((chunks,)), dma((chunks,)), dma((chunks, 2)), dma((chunks,)), dma((chunks,)), dma, dma((experts,)),
            dma((chunks, 2)), dma((chunks, 2)),
            dma((chunks,)), dma((chunks, 2)), dma((chunks,)), dma((chunks, 2)), dma, dma,
        ],
        compiler_params=pltpu.CompilerParams(
            collective_id=0, has_side_effects=True, vmem_limit_bytes=52 * 2**20
        ),
    )(route_ids.T, route_weights.T, out_grad, saved_gate_up, down_weight)
    ggu, gw, ws, gr = (pltpu.with_memory_space_constraint(o, pltpu.VMEM) for o in (ggu, gw, ws, gr))
    ggu, gw, ws, gr = pl.pallas_call(
        store,
        out_shape=tuple(jax.ShapeDtypeStruct(o.shape, o.dtype) for o in (ggu, gw, ws, gr)),
        in_specs=[vmem] * 4,
        out_specs=(hbm,) * 4,
        scratch_shapes=[dma((4,))],
        compiler_params=pltpu.CompilerParams(vmem_limit_bytes=2**20),
    )(ggu, gw, ws, gr)
    return ggu, gw, ws, gr.T


def solution(mesh):
    in_specs = (
        P(("dp", "expert"), None),
        P(("dp", "expert"), None),
        P(("dp", "expert"), None),
        P(("dp", "expert"), None, None),
        P("expert", None, None),
    )
    out_specs = (
        P(("dp", "expert"), None, None),
        P("expert", "dp", None),
        P("expert", "dp", None),
        P(("dp", "expert"), None),
    )
    return jax.shard_map(shards, mesh=mesh, in_specs=in_specs, out_specs=out_specs, check_vma=False)
```
